32 devices in a mesh: rep: 2 (over x), sec: 16 (over z, y, core).
Axes of the slice: x: 2, y: 2, z: 4, core: 2. Of those that a mesh axis runs over, the one named last changes fastest.
Arguments:
- wavefunction: bfloat16 [32, 384, 384], P(('rep', 'sec')), parts along dimension 0, may hold values from -48 to 48
- left_env: bfloat16 [32, 16, 384, 384], P(('rep', 'sec')), parts along dimension 0, may hold values from -3 to 3
- right_env: bfloat16 [32, 16, 384, 384], P(('rep', 'sec')), parts along dimension 0, may hold values from -3 to 3
- sector_sizes: int32 [16, 2], P('sec'), may hold values from 32 to 384, as said below
- term_links: int32 [16, 16], P('sec'), may hold values from 0 to 1, as said below
Outputs:
- applied_first: bfloat16 [32, 384, 384], P(('rep', 'sec')), parts along dimension 0
- applied_second: bfloat16 [32, 384, 384], P(('rep', 'sec')), parts along dimension 0
The draws below stay inside these ranges and needn't reach their ends.
There are 2 independent parts, one for each index of `rep`. The reference program is written for one: setup_inputs(seed, part) draws one part's arguments, and reference() takes and returns one part's arrays. A program takes and returns all parts, laid end to end along the dimension named above; an argument that names none is the same for every part. Nothing has to cross between parts.
Inputs may be any that keep to these rules, and one draw needn't show every extreme that they name: `sector_sizes`: live rows (column 0) and live columns (column 1) of each sector, multiples of 32; one sector has 384 of both and another 32 of both. `term_links`: 0 for every hopping term whose source would leave the down-spin range 0 to 7 or the ends of the sector list.
All inputs are finite; a program needn't handle non-finite values.
Results may differ from the reference program's by a relative error of at most 0.0065.
The reference program's roundings to bfloat16 on the way (of `first_vector`, `product` and `second_vector`) count: a program that leaves them out, or rounds other values in their place, can miss the bound.
Values may be sent and summed in bfloat16 or wider, within the bound.
A program may use at most 128 MiB of HBM per device.

```python
import math
import jax
import jax.numpy as jnp
from jax import lax

BLOCK = 384
ONSITE = 4
HOPS = 3
ND = 8
NSEC = 16
TERMS = 16


def with_energies(noise_part, energy_key):
    energies = jnp.exp(jax.random.uniform(energy_key, (NSEC, TERMS, BLOCK, 1), minval=-0.7, maxval=0.7))
    diag_index = jnp.arange(BLOCK)
    onsite_terms = jnp.arange(TERMS) < ONSITE
    diagonal = (diag_index[:, None] == diag_index[None, :])[None, None] & onsite_terms[None, :, None, None]
    return noise_part * (1.0 / math.sqrt(BLOCK)) + jnp.where(diagonal, energies, 0.0)


def draw_left_env(key, part):
    key = jax.random.fold_in(key, 41)
    noise_key, energy_key = jax.random.split(key)
    block_shape = (NSEC, TERMS, BLOCK, BLOCK)
    noise_part = jnp.clip(jax.random.normal(noise_key, block_shape), -5.0, 5.0)
    return with_energies(noise_part, energy_key).astype(jnp.bfloat16)


def draw_right_env(key, part):
    key = jax.random.fold_in(key, 43)
    noise_key, energy_key = jax.random.split(key)
    block_shape = (NSEC, TERMS, BLOCK, BLOCK)
    noise_part = jnp.clip(jax.random.normal(noise_key, block_shape), -5.0, 5.0)
    return with_energies(noise_part, energy_key).astype(jnp.bfloat16)


def draw_wavefunction(key, part):
    key = jax.random.fold_in(key, 17)
    subkeys = jax.random.split(key, 3)
    block_shape = (NSEC, BLOCK, BLOCK)
    rising = 1.0 + 2.0 * jnp.arange(NSEC, dtype=jnp.float32) / max(NSEC - 1, 1)
    row_scale = jnp.exp(jax.random.uniform(subkeys[1], (NSEC, BLOCK, 1), minval=-1.15, maxval=1.15))
    col_scale = jnp.exp(jax.random.uniform(subkeys[2], (NSEC, 1, BLOCK), minval=-1.15, maxval=1.15))
    entries = jnp.clip(jax.random.normal(subkeys[0], block_shape), -4.0, 4.0)
    factor = 0.3
    return (entries * row_scale * col_scale * rising[:, None, None] * factor).astype(jnp.bfloat16)


def draw_sector_sizes(key, part):
    key = jax.random.fold_in(key, 23)
    subkeys = jax.random.split(key, 2)
    step_count = BLOCK // 32
    lowest_step = max(1, (7 * step_count + 11) // 12)
    live_steps = jax.random.randint(subkeys[0], (NSEC, 2), lowest_step, step_count + 1)
    live_sizes = 32 * live_steps
    shuffled = jax.random.permutation(subkeys[1], NSEC)
    sector_index = jnp.arange(NSEC)[:, None]
    live_sizes = jnp.where(sector_index == shuffled[0], BLOCK, live_sizes)
    live_sizes = jnp.where(sector_index == shuffled[1], 32, live_sizes)
    return live_sizes.astype(jnp.int32)


def draw_term_links(key, part):
    key = jax.random.fold_in(key, 31)
    present = jax.random.randint(key, (NSEC, TERMS), 0, 5) > 0
    sector = jnp.arange(NSEC)[:, None]
    term_index = jnp.arange(TERMS)[None, :]
    direction = jnp.maximum(term_index - ONSITE, 0) // HOPS
    down_value = sector % ND
    inside = jnp.where(direction == 0, down_value > 0, jnp.where(direction == 1, down_value < ND - 1, jnp.where(direction == 2, sector >= ND, sector < NSEC - ND)))
    inside = inside | (term_index < ONSITE)
    return (present & inside).astype(jnp.int32)


def setup_inputs(seed: int = 0, part: int = 0) -> dict:
    streams_of = jax.random.split(jax.random.key(seed), 6)
    part_keys = jax.random.split(jax.random.fold_in(streams_of[5], part), 6)
    wavefunction = draw_wavefunction(jax.random.fold_in(jax.random.fold_in(streams_of[5], part), 71), part)
    left_env = draw_left_env(jax.random.fold_in(jax.random.fold_in(streams_of[5], part), 71), part)
    right_env = draw_right_env(jax.random.fold_in(jax.random.fold_in(streams_of[5], part), 71), part)
    sector_sizes = draw_sector_sizes(jax.random.fold_in(streams_of[5], 71), part)
    term_links = draw_term_links(jax.random.fold_in(streams_of[5], 71), part)
    return {"wavefunction": wavefunction, "left_env": left_env, "right_env": right_env, "sector_sizes": sector_sizes, "term_links": term_links}


def shift_sectors(blocks, offset):
    if offset == 0:
        return blocks
    padding = jnp.zeros((abs(offset),) + blocks.shape[1:], blocks.dtype)
    if offset > 0:
        return jnp.concatenate([padding, blocks[:-offset]], axis=0)
    return jnp.concatenate([blocks[-offset:], padding], axis=0)

def term_offset(term_index):
    if term_index < ONSITE:
        return 0
    return (1, -1, ND, -ND)[(term_index - ONSITE) // HOPS]

def live_mask(sector_sizes):
    positions = jnp.arange(BLOCK, dtype=jnp.int32)
    row_live = positions[None, :, None] < sector_sizes[:, 0][:, None, None]
    col_live = positions[None, None, :] < sector_sizes[:, 1][:, None, None]
    return row_live & col_live

def apply_hamiltonian(vector, left_env, right_env, term_links, live):
    accumulated = jnp.zeros((NSEC, BLOCK, BLOCK), jnp.float32)
    for term_index in range(TERMS):
        offset = term_offset(term_index)
        source = shift_sectors(vector, offset).astype(jnp.float32)
        right_maps = shift_sectors(right_env[:, term_index], offset).astype(jnp.float32)
        product = jnp.einsum('kic,kcd->kid', source, right_maps).astype(jnp.bfloat16)
        product = product * term_links[:, term_index].astype(jnp.bfloat16)[:, None, None]
        left_maps = left_env[:, term_index].astype(jnp.float32)
        accumulated = accumulated + jnp.einsum('kij,kjd->kid', left_maps, product.astype(jnp.float32))
    return jnp.where(live, accumulated, jnp.zeros((), jnp.float32)).astype(jnp.bfloat16)

def reference(wavefunction, left_env, right_env, sector_sizes, term_links):
    live = live_mask(sector_sizes)
    first_vector = jnp.where(live, wavefunction, jnp.zeros((), wavefunction.dtype))
    applied_first = apply_hamiltonian(first_vector, left_env, right_env, term_links, live)
    first_values = first_vector.astype(jnp.float32)
    applied_values = applied_first.astype(jnp.float32)
    correlation = jnp.sum(first_values * applied_values)
    norm_first = jnp.sum(first_values * first_values)
    rayleigh = correlation / (norm_first + 1e-06)
    residual = applied_values - rayleigh * first_values
    spread = jnp.sum(residual * residual)
    second_vector = (residual * lax.rsqrt(spread / (NSEC * BLOCK * BLOCK) + 1e-06)).astype(jnp.bfloat16)
    applied_second = apply_hamiltonian(second_vector, left_env, right_env, term_links, live)
    return (applied_first, applied_second)
```

```python
import functools

import jax
import jax.numpy as jnp
from jax import lax
from jax.experimental import pallas as pl
from jax.experimental.pallas import tpu as pltpu
from jax.sharding import PartitionSpec as P

ONSITE = 4
HOPS = 3
ND = 8
F32 = jnp.float32
BF16 = jnp.bfloat16


def hop_slots(me, sectors):
    down = lax.rem(me, ND)
    base = [ONSITE + HOPS * i for i in range(4)]
    slots = [
        (me - 1, down > 0, me + 1, (down < ND - 1) & (me + 1 < sectors), base[0], base[0]),
        (me + 1, (down < ND - 1) & (me + 1 < sectors), me - 1, down > 0, base[1], base[1]),
    ]
    if sectors == 2 * ND:
        high = me >= ND
        partner = lax.rem(me + ND, sectors)
        slots.append(
            (partner, None, partner, None, jnp.where(high, base[2], base[3]), jnp.where(high, base[3], base[2]))
        )
    else:
        slots.append((me - ND, me >= ND, me + ND, me + ND < sectors, base[2], base[2]))
        slots.append((me + ND, me + ND < sectors, me - ND, me >= ND, base[3], base[3]))
    return slots


def when(condition):
    if condition is None:
        return lambda f: f()
    return pl.when(condition)


def kernel(
    sectors, chunks, sizes_ref, links_ref, wave_hbm, left_hbm, right_hbm,
    first_out, second_out,
    wave, vec, left, right_on, right_hop0, right_hop1, vec_hop, app_hop0, app_hop1, acc_ref, stat_src, stats,
    local_sem, right_send, right_recv, vec_send, vec_recv, app_send, app_recv, stat_send, stat_recv,
):
    me = lax.axis_index("sec")
    block = wave.shape[0]
    slots = hop_slots(me, sectors)
    right_hop = (right_hop0, right_hop1)
    app_hop = (app_hop0, app_hop1)

    load_wave = pltpu.make_async_copy(wave_hbm.at[0], wave, local_sem.at[0])
    load_on = pltpu.make_async_copy(right_hbm.at[0, pl.ds(0, ONSITE)], right_on, local_sem.at[1])
    load_left = pltpu.make_async_copy(left_hbm.at[0], left, local_sem.at[2])
    load_wave.start()
    load_on.start()
    load_left.start()

    barrier = pltpu.get_barrier_semaphore()

    @pl.loop(1, sectors)
    def _(i):
        pl.semaphore_signal(
            barrier, inc=1, device_id={"sec": lax.rem(me + i, sectors)}, device_id_type=pl.DeviceIdType.MESH
        )

    pl.semaphore_wait(barrier, sectors - 1)

    def remote(src, dst, send, recv, device):
        return pltpu.make_async_remote_copy(
            src_ref=src, dst_ref=dst, send_sem=send, recv_sem=recv,
            device_id={"sec": device}, device_id_type=pl.DeviceIdType.MESH,
        )

    def right_copy(s, c):
        start, width = chunks[c]
        return remote(
            right_hbm.at[0, pl.ds(slots[s][5], HOPS), :, pl.ds(start, width)],
            right_hop[c].at[s], right_send.at[s, c], right_recv.at[s, c], slots[s][2],
        )

    def vec_copy(s):
        return remote(vec, vec_hop.at[s], vec_send.at[s], vec_recv.at[s], slots[s][2])

    def app_copy(s, c):
        start, width = chunks[c]
        return remote(
            first_out.at[0, :, pl.ds(start, width)],
            app_hop[c].at[s], app_send.at[s, c], app_recv.at[s, c], slots[s][2],
        )

    order = list(range(len(slots)))[::-1]
    for s in order:
        when(slots[s][3])(lambda s=s: right_copy(s, 0).start())

    load_wave.wait()
    rows_live = sizes_ref[0, 0]
    cols_live = sizes_ref[0, 1]
    row_at = lax.broadcasted_iota(jnp.int32, (block, block), 0)
    col_at = lax.broadcasted_iota(jnp.int32, (block, block), 1)
    live = (row_at < rows_live) & (col_at < cols_live)
    vec[...] = jnp.where(live, wave[...].astype(F32), 0.0).astype(BF16)
    for s in order:
        when(slots[s][3])(lambda s=s: vec_copy(s).start())
    load_on.wait()
    load_left.wait()

    def terms(vector, rights, base, count):
        total = None
        for j in range(count):
            product = jnp.dot(vector, rights(j), preferred_element_type=F32)
            product = (product * links_ref[0, base + j].astype(F32)).astype(BF16)
            part = jnp.dot(left[base + j], product, preferred_element_type=F32)
            total = part if total is None else total + part
        return total

    def onsite(vector_ref, c):
        start, width = chunks[c]
        cols = pl.ds(start, width)
        acc_ref[:, cols] = terms(vector_ref[...], lambda j: right_on[j, :, cols], 0, ONSITE)

    def hop(s, c):
        start, width = chunks[c]
        acc_ref[:, pl.ds(start, width)] += terms(vec_hop[s], lambda j: right_hop[c][s, j], slots[s][4], HOPS)

    def finish(out_ref, c):
        start, width = chunks[c]
        cols = pl.ds(start, width)
        rows = lax.broadcasted_iota(jnp.int32, (block, width), 0)
        at = lax.broadcasted_iota(jnp.int32, (block, width), 1) + start
        region = (rows < rows_live) & (at < cols_live)
        out_ref[0, :, cols] = jnp.where(region, acc_ref[:, cols], 0.0).astype(BF16)

    count = len(slots)
    for c in range(2):
        onsite(vec, c)
    for s in order:
        def next_chunk(s=s):
            right_copy(s, 0).wait_send()
            right_copy(s, 1).start()

        when(slots[s][3])(next_chunk)
    for c in range(2):
        for s in range(count):
            def arrived(s=s, c=c):
                if c == 0:
                    vec_copy(s).wait_recv()
                right_copy(s, c).wait_recv()
                hop(s, c)

            when(slots[s][1])(arrived)
        finish(first_out, c)
        for s in order:
            when(slots[s][3])(lambda s=s, c=c: app_copy(s, c).start())

    v = vec[...].astype(F32)
    a = first_out[0].astype(F32)
    corr = jnp.sum(v * a)
    norm = jnp.sum(v * v)
    local = jnp.full((1, 1), corr, F32) / (jnp.full((1, 1), norm, F32) + 1e-06)
    off = a - local * v
    square = jnp.sum(off * off)
    cross = jnp.sum(off * v)
    row = lax.broadcasted_iota(jnp.int32, (8, 128), 0)
    tile = jnp.where(row == 0, corr, jnp.where(row == 1, norm, jnp.where(row == 2, square, cross)))
    stat_src[...] = jnp.where(row == 4, jnp.broadcast_to(local, (8, 128)), tile)
    stats[me] = stat_src[...]

    def stat_copy(peer, slot):
        return remote(stat_src, stats.at[slot], stat_send.at[peer], stat_recv.at[slot], peer)

    @pl.loop(1, sectors)
    def _(i):
        stat_copy(lax.rem(me + i, sectors), me).start()

    @pl.loop(1, sectors)
    def _(i):
        peer = lax.rem(me + i, sectors)
        stat_copy(peer, peer).wait_recv()

    def column(i):
        return stats[:, i : i + 1, :]

    corr_all = jnp.sum(column(0), axis=0)
    norm_all = jnp.sum(column(1), axis=0)
    ray = corr_all / (norm_all + 1e-06)
    gap = ray[None] - column(4)
    spread = jnp.sum(column(2) - 2.0 * gap * column(3) + gap * gap * column(1), axis=0)
    scale = lax.rsqrt(jnp.maximum(spread, 0.0) / float(sectors * block * block) + 1e-06)
    ray = ray[:, 0:1]
    scale = scale[:, 0:1]

    wave[...] = ((a - ray * v) * scale).astype(BF16)
    for c in range(2):
        onsite(wave, c)
    for s in range(count):
        def again(s=s):
            for c in range(2):
                start, width = chunks[c]
                cols = pl.ds(start, width)
                app_copy(s, c).wait_recv()
                before = vec_hop[s, :, cols].astype(F32)
                vec_hop[s, :, cols] = ((app_hop[c][s].astype(F32) - ray * before) * scale).astype(BF16)
            for c in range(2):
                hop(s, c)

        when(slots[s][1])(again)
    for c in range(2):
        finish(second_out, c)

    for s in order:
        def drain(s=s):
            vec_copy(s).wait_send()
            right_copy(s, 1).wait_send()
            for c in range(2):
                app_copy(s, c).wait_send()

        when(slots[s][3])(drain)

    @pl.loop(1, sectors)
    def _(i):
        stat_copy(lax.rem(me + i, sectors), me).wait_send()


def on_device(sectors, wavefunction, left_env, right_env, sector_sizes, term_links):
    block = wavefunction.shape[1]
    terms = left_env.shape[1]
    split = 256 if block > 256 else block // 2
    chunks = ((0, split), (split, block - split))
    count = 3 if sectors == 2 * ND else 4
    dma = pltpu.SemaphoreType.DMA
    return pl.pallas_call(
        functools.partial(kernel, sectors, chunks),
        out_shape=(jax.ShapeDtypeStruct((1, block, block), BF16),) * 2,
        in_specs=[pl.BlockSpec(memory_space=pltpu.SMEM)] * 2 + [pl.BlockSpec(memory_space=pl.ANY)] * 3,
        out_specs=(pl.BlockSpec(memory_space=pltpu.VMEM),) * 2,
        scratch_shapes=[
            pltpu.VMEM((block, block), BF16),
            pltpu.VMEM((block, block), BF16),
            pltpu.VMEM((terms, block, block), BF16),
            pltpu.VMEM((ONSITE, block, block), BF16),
            pltpu.VMEM((count, HOPS, block, chunks[0][1]), BF16),
            pltpu.VMEM((count, HOPS, block, chunks[1][1]), BF16),
            pltpu.VMEM((count, block, block), BF16),
            pltpu.VMEM((count, block, chunks[0][1]), BF16),
            pltpu.VMEM((count, block, chunks[1][1]), BF16),
            pltpu.VMEM((block, block), F32),
            pltpu.VMEM((8, 128), F32),
            pltpu.VMEM((sectors, 8, 128), F32),
            dma((3,)),
            dma((count, 2)),
            dma((count, 2)),
            dma((count,)),
            dma((count,)),
            dma((count, 2)),
            dma((count, 2)),
            dma((sectors,)),
            dma((sectors,)),
        ],
        compiler_params=pltpu.CompilerParams(
            collective_id=0, has_side_effects=True, vmem_limit_bytes=40 * 1024 * 1024
        ),
        cost_estimate=pl.CostEstimate(
            flops=8 * terms * block**3, bytes_accessed=4 * terms * block * block, transcendentals=0
        ),
    )(sector_sizes, term_links, wavefunction, left_env, right_env)


def solution(mesh):
    return jax.shard_map(
        functools.partial(on_device, mesh.shape["sec"]),
        mesh=mesh,
        in_specs=(
            P(("rep", "sec"), None, None),
            P(("rep", "sec"), None, None, None),
            P(("rep", "sec"), None, None, None),
            P("sec", None),
            P("sec", None),
        ),
        out_specs=(P(("rep", "sec"), None, None), P(("rep", "sec"), None, None)),
        check_vma=False,
    )
```

```python
import functools

import jax
import jax.numpy as jnp
from jax import lax
from jax.experimental import pallas as pl
from jax.experimental.pallas import tpu as pltpu
from jax.sharding import PartitionSpec as P

ONSITE = 4
HOPS = 3
ND = 8
F32 = jnp.float32
BF16 = jnp.bfloat16


def hop_slots(me, sectors):
    down = lax.rem(me, ND)
    base = [ONSITE + HOPS * i for i in range(4)]
    slots = [
        (me - 1, down > 0, me + 1, (down < ND - 1) & (me + 1 < sectors), base[0], base[0]),
        (me + 1, (down < ND - 1) & (me + 1 < sectors), me - 1, down > 0, base[1], base[1]),
    ]
    if sectors == 2 * ND:
        high = me >= ND
        partner = lax.rem(me + ND, sectors)
        slots.append(
            (partner, None, partner, None, jnp.where(high, base[2], base[3]), jnp.where(high, base[3], base[2]))
        )
    else:
        slots.append((me - ND, me >= ND, me + ND, me + ND < sectors, base[2], base[2]))
        slots.append((me + ND, me + ND < sectors, me - ND, me >= ND, base[3], base[3]))
    return slots


def when(condition):
    if condition is None:
        return lambda f: f()
    return pl.when(condition)


def kernel(
    sectors, chunks, sizes_hbm, links_hbm, wave_hbm, left_hbm, right_hbm,
    first_out, second_out,
    sizes_ref, links_ref, wave, vec, left, right_on0, right_on1, right_hop0, right_hop1, vec_hop, app_hop0, app_hop1, acc_ref, stat_src, stats,
    local_sem, left_sem, on_sem, right_send, right_recv, vec_send, vec_recv, app_send, app_recv, stat_send, stat_recv,
):
    me = lax.axis_index("sec")
    block = wave.shape[0]
    slots = hop_slots(me, sectors)
    right_hop = (right_hop0, right_hop1)
    app_hop = (app_hop0, app_hop1)

    count = len(slots)
    wide, narrow = chunks[0][1], chunks[1][1]
    load_wave = pltpu.make_async_copy(wave_hbm.at[0], wave, local_sem.at[0])
    load_sizes = pltpu.make_async_copy(sizes_hbm, sizes_ref, local_sem.at[1])
    load_links = pltpu.make_async_copy(links_hbm, links_ref, local_sem.at[2])
    load_wave.start()
    load_sizes.start()
    load_links.start()
    rest = []
    for w in range(ONSITE):
        rest.append(
            pltpu.make_async_copy(right_hbm.at[0, w, :, pl.ds(0, wide)], right_on0.at[w], on_sem.at[0, w])
        )
        rest.append(
            pltpu.make_async_copy(
                right_hbm.at[0, w, :, pl.ds(wide, narrow)], right_on1.at[:, pl.ds(w * narrow, narrow)], on_sem.at[1, w]
            )
        )
    for w in range(left_hbm.shape[1]):
        rest.append(
            pltpu.make_async_copy(left_hbm.at[0, w], left.at[:, pl.ds(w * block, block)], left_sem.at[w])
        )

    barrier = pltpu.get_barrier_semaphore()

    @pl.loop(1, sectors)
    def _(i):
        pl.semaphore_signal(
            barrier, inc=1, device_id={"sec": lax.rem(me + i, sectors)}, device_id_type=pl.DeviceIdType.MESH
        )

    pl.semaphore_wait(barrier, sectors - 1)

    def remote(src, dst, send, recv, device):
        return pltpu.make_async_remote_copy(
            src_ref=src, dst_ref=dst, send_sem=send, recv_sem=recv,
            device_id={"sec": device}, device_id_type=pl.DeviceIdType.MESH,
        )

    def right_copies(s, c):
        start, width = chunks[c]
        return [
            remote(
                right_hbm.at[0, slots[s][5] + j, :, pl.ds(start, width)],
                right_hop0.at[s, j] if c == 0 else right_hop1.at[s, :, pl.ds(j * width, width)],
                right_send.at[s, c, j], right_recv.at[s, c, j], slots[s][2],
            )
            for j in range(HOPS)
        ]

    def right_start(s, c):
        for copy in right_copies(s, c):
            copy.start()

    def right_sent(s, c):
        for copy in right_copies(s, c):
            copy.wait_send()

    def vec_copy(s):
        return remote(vec, vec_hop.at[s], vec_send.at[s], vec_recv.at[s], slots[s][2])

    def app_copy(s, c):
        start, width = chunks[c]
        return remote(
            first_out.at[0, :, pl.ds(start, width)],
            app_hop[c].at[s], app_send.at[s, c], app_recv.at[s, c], slots[s][2],
        )

    order = list(range(len(slots)))[::-1]
    near, far = range(2), range(2, count)
    for s in far:
        when(slots[s][3])(lambda s=s: right_start(s, 0))

    load_wave.wait()
    load_sizes.wait()
    rows_live = sizes_ref[0, 0]
    cols_live = sizes_ref[0, 1]
    row_at = lax.broadcasted_iota(jnp.int32, (block, block), 0)
    col_at = lax.broadcasted_iota(jnp.int32, (block, block), 1)
    live = (row_at < rows_live) & (col_at < cols_live)
    vec[...] = jnp.where(live, wave[...].astype(F32), 0.0).astype(BF16)
    for s in order:
        when(slots[s][3])(lambda s=s: vec_copy(s).start())
    for s in near:
        def both(s=s):
            right_start(s, 0)
            right_start(s, 1)

        when(slots[s][3])(both)
    for copy in rest:
        copy.start()
    load_links.wait()
    for copy in rest:
        copy.wait()

    def terms(vector, rights, base, number, c):
        if c == 0:
            raw = [jnp.dot(vector, rights[j], preferred_element_type=F32) for j in range(number)]
        else:
            side = jnp.dot(vector, rights[...], preferred_element_type=F32)
            raw = [side[:, j * narrow : (j + 1) * narrow] for j in range(number)]
        products = [(raw[j] * links_ref[0, base + j].astype(F32)).astype(BF16) for j in range(number)]
        at = pl.multiple_of(base * block, 128) if not isinstance(base, int) else base * block
        return jnp.dot(
            left[:, pl.ds(at, number * block)], jnp.concatenate(products, axis=0), preferred_element_type=F32
        )

    def onsite(vector_ref, c):
        start, width = chunks[c]
        rights = right_on0 if c == 0 else right_on1
        acc_ref[:, pl.ds(start, width)] = terms(vector_ref[...], rights, 0, ONSITE, c)

    def hop(s, c):
        start, width = chunks[c]
        acc_ref[:, pl.ds(start, width)] += terms(vec_hop[s], right_hop[c].at[s], slots[s][4], HOPS, c)

    def finish(out_ref, c):
        start, width = chunks[c]
        cols = pl.ds(start, width)
        rows = lax.broadcasted_iota(jnp.int32, (block, width), 0)
        at = lax.broadcasted_iota(jnp.int32, (block, width), 1) + start
        region = (rows < rows_live) & (at < cols_live)
        out_ref[0, :, cols] = jnp.where(region, acc_ref[:, cols], 0.0).astype(BF16)

    for c in range(2):
        onsite(vec, c)
    for s in near:
        def early(s=s):
            vec_copy(s).wait_recv()
            for c in range(2):
                for copy in right_copies(s, c):
                    copy.wait_recv()
                hop(s, c)

        when(slots[s][1])(early)
    for s in far:
        def next_chunk(s=s):
            right_sent(s, 0)
            right_start(s, 1)

        when(slots[s][3])(next_chunk)
    for c in range(2):
        for s in far:
            def arrived(s=s, c=c):
                if c == 0:
                    vec_copy(s).wait_recv()
                for copy in right_copies(s, c):
                    copy.wait_recv()
                hop(s, c)

            when(slots[s][1])(arrived)
        finish(first_out, c)
        for s in order:
            def send(s=s, c=c):
                if c == 0 and s >= 2:
                    right_sent(s, 1)
                app_copy(s, c).start()

            when(slots[s][3])(send)

    v = vec[...].astype(F32)
    a = first_out[0].astype(F32)
    corr = jnp.sum(v * a)
    norm = jnp.sum(v * v)
    local = jnp.full((1, 1), corr, F32) / (jnp.full((1, 1), norm, F32) + 1e-06)
    off = a - local * v
    square = jnp.sum(off * off)
    cross = jnp.sum(off * v)
    row = lax.broadcasted_iota(jnp.int32, (8, 128), 0)
    tile = jnp.where(row == 0, corr, jnp.where(row == 1, norm, jnp.where(row == 2, square, cross)))
    stat_src[...] = jnp.where(row == 4, jnp.broadcast_to(local, (8, 128)), tile)
    stats[me] = stat_src[...]

    def stat_copy(peer, slot):
        return remote(stat_src, stats.at[slot], stat_send.at[peer], stat_recv.at[slot], peer)

    @pl.loop(1, sectors)
    def _(i):
        stat_copy(lax.rem(me + i, sectors), me).start()

    @pl.loop(1, sectors)
    def _(i):
        peer = lax.rem(me + i, sectors)
        stat_copy(peer, peer).wait_recv()

    def column(i):
        return stats[:, i : i + 1, :]

    corr_all = jnp.sum(column(0), axis=0)
    norm_all = jnp.sum(column(1), axis=0)
    ray = corr_all / (norm_all + 1e-06)
    gap = ray[None] - column(4)
    spread = jnp.sum(column(2) - 2.0 * gap * column(3) + gap * gap * column(1), axis=0)
    scale = lax.rsqrt(jnp.maximum(spread, 0.0) / float(sectors * block * block) + 1e-06)
    ray = ray[:, 0:1]
    scale = scale[:, 0:1]

    wave[...] = ((a - ray * v) * scale).astype(BF16)
    for c in range(2):
        onsite(wave, c)
    for s in range(count):
        def again(s=s):
            for c in range(2):
                start, width = chunks[c]
                cols = pl.ds(start, width)
                app_copy(s, c).wait_recv()
                before = vec_hop[s, :, cols].astype(F32)
                vec_hop[s, :, cols] = ((app_hop[c][s].astype(F32) - ray * before) * scale).astype(BF16)
            for c in range(2):
                hop(s, c)

        when(slots[s][1])(again)
    for c in range(2):
        finish(second_out, c)

    for s in order:
        def drain(s=s):
            vec_copy(s).wait_send()
            if s < 2:
                right_sent(s, 0)
                right_sent(s, 1)
            for c in range(2):
                app_copy(s, c).wait_send()

        when(slots[s][3])(drain)

    @pl.loop(1, sectors)
    def _(i):
        stat_copy(lax.rem(me + i, sectors), me).wait_send()


def on_device(sectors, wavefunction, left_env, right_env, sector_sizes, term_links):
    block = wavefunction.shape[1]
    terms = left_env.shape[1]
    split = 256 if block > 256 else block // 2
    chunks = ((0, split), (split, block - split))
    count = 3 if sectors == 2 * ND else 4
    dma = pltpu.SemaphoreType.DMA
    return pl.pallas_call(
        functools.partial(kernel, sectors, chunks),
        out_shape=(jax.ShapeDtypeStruct((1, block, block), BF16),) * 2,
        in_specs=[pl.BlockSpec(memory_space=pltpu.HBM)] * 5,
        out_specs=(pl.BlockSpec(memory_space=pltpu.VMEM),) * 2,
        scratch_shapes=[
            pltpu.SMEM(sector_sizes.shape, jnp.int32),
            pltpu.SMEM(term_links.shape, jnp.int32),
            pltpu.VMEM((block, block), BF16),
            pltpu.VMEM((block, block), BF16),
            pltpu.VMEM((block, terms * block), BF16),
            pltpu.VMEM((ONSITE, block, chunks[0][1]), BF16),
            pltpu.VMEM((block, ONSITE * chunks[1][1]), BF16),
            pltpu.VMEM((count, HOPS, block, chunks[0][1]), BF16),
            pltpu.VMEM((count, block, HOPS * chunks[1][1]), BF16),
            pltpu.VMEM((count, block, block), BF16),
            pltpu.VMEM((count, block, chunks[0][1]), BF16),
            pltpu.VMEM((count, block, chunks[1][1]), BF16),
            pltpu.VMEM((block, block), F32),
            pltpu.VMEM((8, 128), F32),
            pltpu.VMEM((sectors, 8, 128), F32),
            dma((3,)),
            dma((terms,)),
            dma((2, ONSITE)),
            dma((count, 2, HOPS)),
            dma((count, 2, HOPS)),
            dma((count,)),
            dma((count,)),
            dma((count, 2)),
            dma((count, 2)),
            dma((sectors,)),
            dma((sectors,)),
        ],
        compiler_params=pltpu.CompilerParams(
            collective_id=0, has_side_effects=True, vmem_limit_bytes=int(63.0 * 1024 * 1024)
        ),
        cost_estimate=pl.CostEstimate(
            flops=8 * terms * block**3, bytes_accessed=4 * terms * block * block, transcendentals=0
        ),
    )(sector_sizes, term_links, wavefunction, left_env, right_env)


def solution(mesh):
    return jax.shard_map(
        functools.partial(on_device, mesh.shape["sec"]),
        mesh=mesh,
        in_specs=(
            P(("rep", "sec"), None, None),
            P(("rep", "sec"), None, None, None),
            P(("rep", "sec"), None, None, None),
            P("sec", None),
            P("sec", None),
        ),
        out_specs=(P(("rep", "sec"), None, None), P(("rep", "sec"), None, None)),
        check_vma=False,
    )
```

```python
import functools

import jax
import jax.numpy as jnp
from jax import lax
from jax.experimental import pallas as pl
from jax.experimental.pallas import tpu as pltpu
from jax.sharding import PartitionSpec as P

ONSITE = 4
HOPS = 3
ND = 8
F32 = jnp.float32
BF16 = jnp.bfloat16


def hop_slots(me, sectors):
    down = lax.rem(me, ND)
    base = [ONSITE + HOPS * i for i in range(4)]
    slots = [
        (me - 1, down > 0, me + 1, (down < ND - 1) & (me + 1 < sectors), base[0], base[0]),
        (me + 1, (down < ND - 1) & (me + 1 < sectors), me - 1, down > 0, base[1], base[1]),
    ]
    if sectors == 2 * ND:
        high = me >= ND
        partner = lax.rem(me + ND, sectors)
        slots.append(
            (partner, None, partner, None, jnp.where(high, base[2], base[3]), jnp.where(high, base[3], base[2]))
        )
    else:
        slots.append((me - ND, me >= ND, me + ND, me + ND < sectors, base[2], base[2]))
        slots.append((me + ND, me + ND < sectors, me - ND, me >= ND, base[3], base[3]))
    return slots


def when(condition):
    if condition is None:
        return lambda f: f()
    return pl.when(condition)


def kernel(
    sectors, chunks, sizes_hbm, links_hbm, wave_hbm, left_hbm, right_hbm,
    first_hbm, second_hbm,
    first_out, second_out,
    sizes_ref, links_ref, wave, vec, left, right_on0, right_on1, right_hop0, right_hop1, vec_hop, app_hop0, app_hop1, acc_ref, stat_src, stats,
    local_sem, out_sem, left_sem, on_sem, right_send, right_recv, vec_send, vec_recv, app_send, app_recv, stat_send, stat_recv,
):
    me = lax.axis_index("sec")
    block = wave.shape[0]
    slots = hop_slots(me, sectors)
    right_hop = (right_hop0, right_hop1)
    app_hop = (app_hop0, app_hop1)

    wide, narrow = chunks[0][1], chunks[1][1]
    count = len(slots)
    load_wave = pltpu.make_async_copy(wave_hbm.at[0], wave, local_sem.at[0])
    load_sizes = pltpu.make_async_copy(sizes_hbm, sizes_ref, local_sem.at[1])
    load_links = pltpu.make_async_copy(links_hbm, links_ref, local_sem.at[2])
    load_wave.start()
    load_sizes.start()
    load_links.start()
    rest = []
    for w in range(ONSITE):
        rest.append(
            pltpu.make_async_copy(right_hbm.at[0, w, :, pl.ds(0, wide)], right_on0.at[w], on_sem.at[0, w])
        )
        rest.append(
            pltpu.make_async_copy(
                right_hbm.at[0, w, :, pl.ds(wide, narrow)], right_on1.at[:, pl.ds(w * narrow, narrow)], on_sem.at[1, w]
            )
        )
    for w in range(left_hbm.shape[1]):
        rest.append(
            pltpu.make_async_copy(left_hbm.at[0, w], left.at[:, pl.ds(w * block, block)], left_sem.at[w])
        )

    barrier = pltpu.get_barrier_semaphore()

    @pl.loop(1, sectors)
    def _(i):
        pl.semaphore_signal(
            barrier, inc=1, device_id={"sec": lax.rem(me + i, sectors)}, device_id_type=pl.DeviceIdType.MESH
        )

    pl.semaphore_wait(barrier, sectors - 1)

    def remote(src, dst, send, recv, device):
        return pltpu.make_async_remote_copy(
            src_ref=src, dst_ref=dst, send_sem=send, recv_sem=recv,
            device_id={"sec": device}, device_id_type=pl.DeviceIdType.MESH,
        )

    def right_copies(s, c):
        start, width = chunks[c]
        return [
            remote(
                right_hbm.at[0, slots[s][5] + j, :, pl.ds(start, width)],
                right_hop0.at[s, j] if c == 0 else right_hop1.at[s, :, pl.ds(j * width, width)],
                right_send.at[s, c, j], right_recv.at[s, c, j], slots[s][2],
            )
            for j in range(HOPS)
        ]

    def right_start(s, c):
        for copy in right_copies(s, c):
            copy.start()

    def right_sent(s, c):
        for copy in right_copies(s, c):
            copy.wait_send()

    def vec_copy(s):
        return remote(vec, vec_hop.at[s], vec_send.at[s], vec_recv.at[s], slots[s][2])

    def app_copy(s, c):
        start, width = chunks[c]
        return remote(
            first_out.at[0, :, pl.ds(start, width)],
            app_hop[c].at[s], app_send.at[s, c], app_recv.at[s, c], slots[s][2],
        )

    order = list(range(len(slots)))[::-1]
    near, far = range(2), range(2, count)
    for s in far:
        when(slots[s][3])(lambda s=s: right_start(s, 0))

    load_wave.wait()
    load_sizes.wait()
    rows_live = sizes_ref[0, 0]
    cols_live = sizes_ref[0, 1]
    row_at = lax.broadcasted_iota(jnp.int32, (block, block), 0)
    col_at = lax.broadcasted_iota(jnp.int32, (block, block), 1)
    live = (row_at < rows_live) & (col_at < cols_live)
    vec[...] = jnp.where(live, wave[...].astype(F32), 0.0).astype(BF16)
    for s in order:
        when(slots[s][3])(lambda s=s: vec_copy(s).start())
    for s in near:
        def both(s=s):
            right_start(s, 0)
            right_start(s, 1)

        when(slots[s][3])(both)
    for copy in rest:
        copy.start()
    load_links.wait()
    for copy in rest:
        copy.wait()

    def terms(vector, rights, base, number, c):
        if c == 0:
            raw = [jnp.dot(vector, rights[j], preferred_element_type=F32) for j in range(number)]
        else:
            side = jnp.dot(vector, rights[...], preferred_element_type=F32)
            raw = [side[:, j * narrow : (j + 1) * narrow] for j in range(number)]
        products = [(raw[j] * links_ref[0, base + j].astype(F32)).astype(BF16) for j in range(number)]
        at = pl.multiple_of(base * block, 128) if not isinstance(base, int) else base * block
        return jnp.dot(
            left[:, pl.ds(at, number * block)], jnp.concatenate(products, axis=0), preferred_element_type=F32
        )

    def onsite(vector_ref, c):
        start, width = chunks[c]
        rights = right_on0 if c == 0 else right_on1
        acc_ref[:, pl.ds(start, width)] = terms(vector_ref[...], rights, 0, ONSITE, c)

    def hop(s, c):
        start, width = chunks[c]
        acc_ref[:, pl.ds(start, width)] += terms(vec_hop[s], right_hop[c].at[s], slots[s][4], HOPS, c)

    def finish(out_ref, c):
        start, width = chunks[c]
        cols = pl.ds(start, width)
        rows = lax.broadcasted_iota(jnp.int32, (block, width), 0)
        at = lax.broadcasted_iota(jnp.int32, (block, width), 1) + start
        region = (rows < rows_live) & (at < cols_live)
        out_ref[0, :, cols] = jnp.where(region, acc_ref[:, cols], 0.0).astype(BF16)

    def sums(c, about):
        start, width = chunks[c]
        v = vec[:, pl.ds(start, width)].astype(F32)
        a = first_out[0, :, pl.ds(start, width)].astype(F32)
        corr = jnp.sum(v * a, keepdims=True)
        norm = jnp.sum(v * v, keepdims=True)
        if about is None:
            return corr, norm, None, None
        off = a - about * v
        return corr, norm, jnp.sum(off * off, keepdims=True), jnp.sum(off * v, keepdims=True)

    for c in range(2):
        onsite(vec, c)
    for s in near:
        def early(s=s):
            vec_copy(s).wait_recv()
            for c in range(2):
                for copy in right_copies(s, c):
                    copy.wait_recv()
                hop(s, c)

        when(slots[s][1])(early)
    for s in far:
        def next_chunk(s=s):
            right_sent(s, 0)
            right_start(s, 1)

        when(slots[s][3])(next_chunk)
    for c in range(2):
        for s in far:
            def arrived(s=s, c=c):
                if c == 0:
                    vec_copy(s).wait_recv()
                for copy in right_copies(s, c):
                    copy.wait_recv()
                hop(s, c)

            when(slots[s][1])(arrived)
        finish(first_out, c)
        if c == 1:
            for s in near:
                when(slots[s][3])(lambda s=s: app_copy(s, 1).start())
            break
        for s in order:
            def send(s=s):
                if s < 2:
                    app_copy(s, 0).start()

            when(slots[s][3])(send)
        corr, norm, _, _ = sums(c, None)
        local = corr / (norm + 1e-06)
        first_sums = sums(c, local)

    corr, norm, square, cross = (x + y for x, y in zip(first_sums, sums(1, local)))
    lane = lax.broadcasted_iota(jnp.int32, (1, 128), 1)
    tile = jnp.where(lane == 4, local, cross)
    for i, value in enumerate((corr, norm, square)):
        tile = jnp.where(lane == i, value, tile)
    stat_src[...] = tile
    stats[me] = tile

    def stat_copy(peer, slot):
        return remote(stat_src, stats.at[slot], stat_send.at[peer], stat_recv.at[slot], peer)

    @pl.loop(1, sectors)
    def _(i):
        stat_copy(lax.rem(me + i, sectors), me).start()

    for s in far:
        def late(s=s):
            app_copy(s, 0).start()
            app_copy(s, 1).start()

        when(slots[s][3])(late)
    first_write = pltpu.make_async_copy(first_out, first_hbm, out_sem.at[0])
    first_write.start()

    @pl.loop(1, sectors)
    def _(i):
        peer = lax.rem(me + i, sectors)
        stat_copy(peer, peer).wait_recv()

    def column(i):
        return jnp.sum(jnp.where(lane[None] == i, stats[...], 0.0), axis=2, keepdims=True)

    corr_all = jnp.sum(column(0), axis=0)
    norm_all = jnp.sum(column(1), axis=0)
    ray = corr_all / (norm_all + 1e-06)
    gap = ray[None] - column(4)
    spread = jnp.sum(column(2) - 2.0 * gap * column(3) + gap * gap * column(1), axis=0)
    scale = lax.rsqrt(jnp.maximum(spread, 0.0) / float(sectors * block * block) + 1e-06)

    v = vec[...].astype(F32)
    a = first_out[0].astype(F32)
    wave[...] = ((a - ray * v) * scale).astype(BF16)
    for c in range(2):
        onsite(wave, c)
    for s in range(count):
        def again(s=s):
            for c in range(2):
                start, width = chunks[c]
                cols = pl.ds(start, width)
                app_copy(s, c).wait_recv()
                before = vec_hop[s, :, cols].astype(F32)
                vec_hop[s, :, cols] = ((app_hop[c][s].astype(F32) - ray * before) * scale).astype(BF16)
            for c in range(2):
                hop(s, c)

        when(slots[s][1])(again)
    second_writes = []
    for c in range(2):
        start, width = chunks[c]
        finish(second_out, c)
        second_writes.append(
            pltpu.make_async_copy(
                second_out.at[:, :, pl.ds(start, width)], second_hbm.at[:, :, pl.ds(start, width)], out_sem.at[1 + c]
            )
        )
        second_writes[c].start()

    for s in order:
        def drain(s=s):
            vec_copy(s).wait_send()
            if s < 2:
                right_sent(s, 0)
            right_sent(s, 1)
            for c in range(2):
                app_copy(s, c).wait_send()

        when(slots[s][3])(drain)

    @pl.loop(1, sectors)
    def _(i):
        stat_copy(lax.rem(me + i, sectors), me).wait_send()

    first_write.wait()
    for write in second_writes:
        write.wait()


def settle_kernel(first_in, second_in, first_hbm, second_hbm, held, sem):
    inward = [
        pltpu.make_async_copy(first_in, held.at[0], sem.at[0]),
        pltpu.make_async_copy(second_in, held.at[1], sem.at[1]),
    ]
    outward = [
        pltpu.make_async_copy(held.at[0], first_hbm, sem.at[2]),
        pltpu.make_async_copy(held.at[1], second_hbm, sem.at[3]),
    ]
    for copy in inward:
        copy.start()
    for i in range(2):
        inward[i].wait()
        outward[i].start()
    for copy in outward:
        copy.wait()


def settle(first, second):
    hbm = pl.BlockSpec(memory_space=pltpu.HBM)
    return pl.pallas_call(
        settle_kernel,
        out_shape=(jax.ShapeDtypeStruct(first.shape, BF16),) * 2,
        in_specs=[hbm, hbm],
        out_specs=(hbm, hbm),
        scratch_shapes=[pltpu.VMEM((2,) + first.shape, BF16), pltpu.SemaphoreType.DMA((4,))],
        compiler_params=pltpu.CompilerParams(vmem_limit_bytes=63 * 1024 * 1024),
    )(first, second)


def on_device(sectors, wavefunction, left_env, right_env, sector_sizes, term_links):
    block = wavefunction.shape[1]
    terms = left_env.shape[1]
    split = 256 if block > 256 else block // 2
    chunks = ((0, split), (split, block - split))
    count = 3 if sectors == 2 * ND else 4
    dma = pltpu.SemaphoreType.DMA
    first, second = pl.pallas_call(
        functools.partial(kernel, sectors, chunks),
        out_shape=(jax.ShapeDtypeStruct((1, block, block), BF16),) * 2,
        in_specs=[pl.BlockSpec(memory_space=pltpu.HBM)] * 5,
        out_specs=(pl.BlockSpec(memory_space=pltpu.HBM),) * 2,
        scratch_shapes=[
            pltpu.VMEM((1, block, block), BF16),
            pltpu.VMEM((1, block, block), BF16),
            pltpu.SMEM(sector_sizes.shape, jnp.int32),
            pltpu.SMEM(term_links.shape, jnp.int32),
            pltpu.VMEM((block, block), BF16),
            pltpu.VMEM((block, block), BF16),
            pltpu.VMEM((block, terms * block), BF16),
            pltpu.VMEM((ONSITE, block, chunks[0][1]), BF16),
            pltpu.VMEM((block, ONSITE * chunks[1][1]), BF16),
            pltpu.VMEM((count, HOPS, block, chunks[0][1]), BF16),
            pltpu.VMEM((count, block, HOPS * chunks[1][1]), BF16),
            pltpu.VMEM((count, block, block), BF16),
            pltpu.VMEM((count, block, chunks[0][1]), BF16),
            pltpu.VMEM((count, block, chunks[1][1]), BF16),
            pltpu.VMEM((block, block), F32),
            pltpu.VMEM((1, 128), F32),
            pltpu.VMEM((sectors, 1, 128), F32),
            dma((3,)),
            dma((3,)),
            dma((terms,)),
            dma((2, ONSITE)),
            dma((count, 2, HOPS)),
            dma((count, 2, HOPS)),
            dma((count,)),
            dma((count,)),
            dma((count, 2)),
            dma((count, 2)),
            dma((sectors,)),
            dma((sectors,)),
        ],
        compiler_params=pltpu.CompilerParams(
            collective_id=0, has_side_effects=True, vmem_limit_bytes=int(63.0 * 1024 * 1024)
        ),
        cost_estimate=pl.CostEstimate(
            flops=8 * terms * block**3, bytes_accessed=4 * terms * block * block, transcendentals=0
        ),
    )(sector_sizes, term_links, wavefunction, left_env, right_env)
    return settle(first, second)


def solution(mesh):
    return jax.shard_map(
        functools.partial(on_device, mesh.shape["sec"]),
        mesh=mesh,
        in_specs=(
            P(("rep", "sec"), None, None),
            P(("rep", "sec"), None, None, None),
            P(("rep", "sec"), None, None, None),
            P("sec", None),
            P("sec", None),
        ),
        out_specs=(P(("rep", "sec"), None, None), P(("rep", "sec"), None, None)),
        check_vma=False,
    )
```

```python
import functools

import jax
import jax.numpy as jnp
from jax import lax
from jax.experimental import pallas as pl
from jax.experimental.pallas import tpu as pltpu
from jax.sharding import PartitionSpec as P

ONSITE = 4
HOPS = 3
ND = 8
F32 = jnp.float32
BF16 = jnp.bfloat16


def hop_slots(me, sectors):
    down = lax.rem(me, ND)
    base = [ONSITE + HOPS * i for i in range(4)]
    slots = [
        (me - 1, down > 0, me + 1, (down < ND - 1) & (me + 1 < sectors), base[0], base[0]),
        (me + 1, (down < ND - 1) & (me + 1 < sectors), me - 1, down > 0, base[1], base[1]),
    ]
    if sectors == 2 * ND:
        high = me >= ND
        partner = lax.rem(me + ND, sectors)
        slots.append(
            (partner, None, partner, None, jnp.where(high, base[2], base[3]), jnp.where(high, base[3], base[2]))
        )
    else:
        slots.append((me - ND, me >= ND, me + ND, me + ND < sectors, base[2], base[2]))
        slots.append((me + ND, me + ND < sectors, me - ND, me >= ND, base[3], base[3]))
    return slots


def when(condition):
    if condition is None:
        return lambda f: f()
    return pl.when(condition)


def kernel(
    sectors, chunks, sizes_hbm, links_hbm, wave_hbm, left_hbm, right_hbm,
    first_hbm, second_hbm,
    first_out, second_out,
    sizes_ref, links_ref, wave, vec, left, right_on0, right_on1, right_hop0, right_hop1, vec_hop, app_hop, acc_ref, stat_src, stats,
    local_sem, out_sem, left_sem, on_sem, right_send, right_recv, vec_send, vec_recv, app_send, app_recv, stat_send, stat_recv,
):
    me = lax.axis_index("sec")
    block = wave.shape[0]
    slots = hop_slots(me, sectors)
    right_hop = (right_hop0, right_hop1)

    wide, narrow = chunks[0][1], chunks[1][1]
    count = len(slots)
    load_wave = pltpu.make_async_copy(wave_hbm.at[0], wave, local_sem.at[0])
    load_sizes = pltpu.make_async_copy(sizes_hbm, sizes_ref, local_sem.at[1])
    load_links = pltpu.make_async_copy(links_hbm, links_ref, local_sem.at[2])
    load_wave.start()
    load_sizes.start()
    load_links.start()
    rest = []
    for w in range(ONSITE):
        rest.append(
            pltpu.make_async_copy(right_hbm.at[0, w, :, pl.ds(0, wide)], right_on0.at[w], on_sem.at[0, w])
        )
        rest.append(
            pltpu.make_async_copy(
                right_hbm.at[0, w, :, pl.ds(wide, narrow)], right_on1.at[:, pl.ds(w * narrow, narrow)], on_sem.at[1, w]
            )
        )
    for w in range(left_hbm.shape[1]):
        rest.append(
            pltpu.make_async_copy(left_hbm.at[0, w], left.at[:, pl.ds(w * block, block)], left_sem.at[w])
        )

    barrier = pltpu.get_barrier_semaphore()

    @pl.loop(1, sectors)
    def _(i):
        pl.semaphore_signal(
            barrier, inc=1, device_id={"sec": lax.rem(me + i, sectors)}, device_id_type=pl.DeviceIdType.MESH
        )

    pl.semaphore_wait(barrier, sectors - 1)

    def remote(src, dst, send, recv, device):
        return pltpu.make_async_remote_copy(
            src_ref=src, dst_ref=dst, send_sem=send, recv_sem=recv,
            device_id={"sec": device}, device_id_type=pl.DeviceIdType.MESH,
        )

    def right_copies(s, c):
        start, width = chunks[c]
        return [
            remote(
                right_hbm.at[0, slots[s][5] + j, :, pl.ds(start, width)],
                right_hop0.at[s, j] if c == 0 else right_hop1.at[s, :, pl.ds(j * width, width)],
                right_send.at[s, c, j], right_recv.at[s, c, j], slots[s][2],
            )
            for j in range(HOPS)
        ]

    def right_start(s, c):
        for copy in right_copies(s, c):
            copy.start()

    def right_sent(s, c):
        for copy in right_copies(s, c):
            copy.wait_send()

    def vec_copy(s):
        return remote(vec, vec_hop.at[s], vec_send.at[s], vec_recv.at[s], slots[s][2])

    pieces = ((0, narrow), (narrow, wide - narrow), (wide, narrow))

    def app_copy(s, p):
        start, width = pieces[p]
        return remote(
            first_out.at[0, :, pl.ds(start, width)], app_hop.at[s, :, pl.ds(start, width)],
            app_send.at[s, p], app_recv.at[s, p], slots[s][2],
        )

    order = list(range(len(slots)))[::-1]
    near, far = range(2), range(2, count)
    for s in far:
        when(slots[s][3])(lambda s=s: right_start(s, 0))

    load_wave.wait()
    load_sizes.wait()
    rows_live = sizes_ref[0, 0]
    cols_live = sizes_ref[0, 1]
    row_at = lax.broadcasted_iota(jnp.int32, (block, block), 0)
    col_at = lax.broadcasted_iota(jnp.int32, (block, block), 1)
    live = (row_at < rows_live) & (col_at < cols_live)
    vec[...] = jnp.where(live, wave[...].astype(F32), 0.0).astype(BF16)
    for s in order:
        when(slots[s][3])(lambda s=s: vec_copy(s).start())
    for s in near:
        def both(s=s):
            right_start(s, 0)
            right_start(s, 1)

        when(slots[s][3])(both)
    for copy in rest:
        copy.start()
    load_links.wait()
    for copy in rest:
        copy.wait()

    def terms(vector, rights, base, number, c, skip=0):
        if c == 0:
            raw = [jnp.dot(vector, rights[j], preferred_element_type=F32) for j in range(number)]
        else:
            side = jnp.dot(
                vector, rights[:, pl.ds(skip * narrow, number * narrow)], preferred_element_type=F32
            )
            raw = [side[:, j * narrow : (j + 1) * narrow] for j in range(number)]
        base = base + skip
        products = [(raw[j] * links_ref[0, base + j].astype(F32)).astype(BF16) for j in range(number)]
        at = pl.multiple_of(base * block, 128) if not isinstance(base, int) else base * block
        return jnp.dot(
            left[:, pl.ds(at, number * block)], jnp.concatenate(products, axis=0), preferred_element_type=F32
        )

    def onsite(vector_ref, c):
        start, width = chunks[c]
        rights = right_on0 if c == 0 else right_on1
        acc_ref[:, pl.ds(start, width)] = terms(vector_ref[...], rights, 0, ONSITE, c)

    def hop(s, c, number=HOPS, skip=0):
        start, width = chunks[c]
        acc_ref[:, pl.ds(start, width)] += terms(vec_hop[s], right_hop[c].at[s], slots[s][4], number, c, skip)

    def finish(out_ref, c):
        start, width = chunks[c]
        cols = pl.ds(start, width)
        rows = lax.broadcasted_iota(jnp.int32, (block, width), 0)
        at = lax.broadcasted_iota(jnp.int32, (block, width), 1) + start
        region = (rows < rows_live) & (at < cols_live)
        out_ref[0, :, cols] = jnp.where(region, acc_ref[:, cols], 0.0).astype(BF16)

    def sums(c, about):
        start, width = chunks[c]
        v = vec[:, pl.ds(start, width)].astype(F32)
        a = first_out[0, :, pl.ds(start, width)].astype(F32)
        corr = jnp.sum(v * a, keepdims=True)
        norm = jnp.sum(v * v, keepdims=True)
        if about is None:
            return corr, norm, None, None
        off = a - about * v
        return corr, norm, jnp.sum(off * off, keepdims=True), jnp.sum(off * v, keepdims=True)

    for c in range(2):
        onsite(vec, c)
    for s in near:
        def early(s=s):
            vec_copy(s).wait_recv()
            for c in range(2):
                for copy in right_copies(s, c):
                    copy.wait_recv()
                hop(s, c)

        when(slots[s][1])(early)
    for s in far:
        def next_chunk(s=s):
            right_sent(s, 0)
            right_start(s, 1)

        when(slots[s][3])(next_chunk)
    for c in range(2):
        for s in far:
            def arrived(s=s, c=c):
                copies = right_copies(s, c)
                if c == 0:
                    vec_copy(s).wait_recv()
                    for copy in copies:
                        copy.wait_recv()
                    hop(s, c)
                else:
                    for copy in copies[:-1]:
                        copy.wait_recv()
                    hop(s, c, HOPS - 1)
                    copies[-1].wait_recv()

            when(slots[s][1])(arrived)
        if c == 1:
            for s in far:
                when(slots[s][3])(lambda s=s: app_copy(s, 0).start())
            for s in far:
                when(slots[s][1])(lambda s=s: hop(s, 1, 1, HOPS - 1))
        finish(first_out, c)
        if c == 1:
            for s in near:
                when(slots[s][3])(lambda s=s: app_copy(s, 2).start())
            break
        for s in order:
            def send(s=s):
                if s < 2:
                    app_copy(s, 0).start()
                    app_copy(s, 1).start()

            when(slots[s][3])(send)
        corr, norm, _, _ = sums(c, None)
        local = corr / (norm + 1e-06)
        first_sums = sums(c, local)

    corr, norm, square, cross = (x + y for x, y in zip(first_sums, sums(1, local)))
    lane = lax.broadcasted_iota(jnp.int32, (1, 128), 1)
    tile = jnp.where(lane == 4, local, cross)
    for i, value in enumerate((corr, norm, square)):
        tile = jnp.where(lane == i, value, tile)
    stat_src[...] = tile
    stats[me] = tile

    def stat_copy(peer, slot):
        return remote(stat_src, stats.at[slot], stat_send.at[peer], stat_recv.at[slot], peer)

    @pl.loop(1, sectors)
    def _(i):
        stat_copy(lax.rem(me + i, sectors), me).start()

    for s in far:
        def late(s=s):
            app_copy(s, 1).start()
            app_copy(s, 2).start()

        when(slots[s][3])(late)
    first_write = pltpu.make_async_copy(first_out, first_hbm, out_sem.at[0])
    first_write.start()

    @pl.loop(1, sectors)
    def _(i):
        peer = lax.rem(me + i, sectors)
        stat_copy(peer, peer).wait_recv()

    def column(i):
        return jnp.sum(jnp.where(lane[None] == i, stats[...], 0.0), axis=2, keepdims=True)

    corr_all = jnp.sum(column(0), axis=0)
    norm_all = jnp.sum(column(1), axis=0)
    ray = corr_all / (norm_all + 1e-06)
    gap = ray[None] - column(4)
    spread = jnp.sum(column(2) - 2.0 * gap * column(3) + gap * gap * column(1), axis=0)
    scale = lax.rsqrt(jnp.maximum(spread, 0.0) / float(sectors * block * block) + 1e-06)

    v = vec[...].astype(F32)
    a = first_out[0].astype(F32)
    wave[...] = ((a - ray * v) * scale).astype(BF16)
    for c in range(2):
        onsite(wave, c)
    for s in range(count):
        def again(s=s):
            for p in range(3):
                app_copy(s, p).wait_recv()
            before = vec_hop[s].astype(F32)
            vec_hop[s] = ((app_hop[s].astype(F32) - ray * before) * scale).astype(BF16)
            for c in range(2):
                hop(s, c)

        when(slots[s][1])(again)
    second_writes = []
    for c in range(2):
        start, width = chunks[c]
        finish(second_out, c)
        second_writes.append(
            pltpu.make_async_copy(
                second_out.at[:, :, pl.ds(start, width)], second_hbm.at[:, :, pl.ds(start, width)], out_sem.at[1 + c]
            )
        )
        second_writes[c].start()

    for s in order:
        def drain(s=s):
            vec_copy(s).wait_send()
            if s < 2:
                right_sent(s, 0)
            right_sent(s, 1)
            for p in range(3):
                app_copy(s, p).wait_send()

        when(slots[s][3])(drain)

    @pl.loop(1, sectors)
    def _(i):
        stat_copy(lax.rem(me + i, sectors), me).wait_send()

    first_write.wait()
    for write in second_writes:
        write.wait()


def settle_kernel(first_in, second_in, first_hbm, second_hbm, held, sem):
    inward = [
        pltpu.make_async_copy(first_in, held.at[0], sem.at[0]),
        pltpu.make_async_copy(second_in, held.at[1], sem.at[1]),
    ]
    outward = [
        pltpu.make_async_copy(held.at[0], first_hbm, sem.at[2]),
        pltpu.make_async_copy(held.at[1], second_hbm, sem.at[3]),
    ]
    for copy in inward:
        copy.start()
    for i in range(2):
        inward[i].wait()
        outward[i].start()
    for copy in outward:
        copy.wait()


def settle(first, second):
    hbm = pl.BlockSpec(memory_space=pltpu.HBM)
    return pl.pallas_call(
        settle_kernel,
        out_shape=(jax.ShapeDtypeStruct(first.shape, BF16),) * 2,
        in_specs=[hbm, hbm],
        out_specs=(hbm, hbm),
        scratch_shapes=[pltpu.VMEM((2,) + first.shape, BF16), pltpu.SemaphoreType.DMA((4,))],
        compiler_params=pltpu.CompilerParams(vmem_limit_bytes=63 * 1024 * 1024),
    )(first, second)


def on_device(sectors, wavefunction, left_env, right_env, sector_sizes, term_links):
    block = wavefunction.shape[1]
    terms = left_env.shape[1]
    split = 256 if block > 256 else block // 2
    chunks = ((0, split), (split, block - split))
    count = 3 if sectors == 2 * ND else 4
    dma = pltpu.SemaphoreType.DMA
    first, second = pl.pallas_call(
        functools.partial(kernel, sectors, chunks),
        out_shape=(jax.ShapeDtypeStruct((1, block, block), BF16),) * 2,
        in_specs=[pl.BlockSpec(memory_space=pltpu.HBM)] * 5,
        out_specs=(pl.BlockSpec(memory_space=pltpu.HBM),) * 2,
        scratch_shapes=[
            pltpu.VMEM((1, block, block), BF16),
            pltpu.VMEM((1, block, block), BF16),
            pltpu.SMEM(sector_sizes.shape, jnp.int32),
            pltpu.SMEM(term_links.shape, jnp.int32),
            pltpu.VMEM((block, block), BF16),
            pltpu.VMEM((block, block), BF16),
            pltpu.VMEM((block, terms * block), BF16),
            pltpu.VMEM((ONSITE, block, chunks[0][1]), BF16),
            pltpu.VMEM((block, ONSITE * chunks[1][1]), BF16),
            pltpu.VMEM((count, HOPS, block, chunks[0][1]), BF16),
            pltpu.VMEM((count, block, HOPS * chunks[1][1]), BF16),
            pltpu.VMEM((count, block, block), BF16),
            pltpu.VMEM((count, block, block), BF16),
            pltpu.VMEM((block, block), F32),
            pltpu.VMEM((1, 128), F32),
            pltpu.VMEM((sectors, 1, 128), F32),
            dma((3,)),
            dma((3,)),
            dma((terms,)),
            dma((2, ONSITE)),
            dma((count, 2, HOPS)),
            dma((count, 2, HOPS)),
            dma((count,)),
            dma((count,)),
            dma((count, 3)),
            dma((count, 3)),
            dma((sectors,)),
            dma((sectors,)),
        ],
        compiler_params=pltpu.CompilerParams(
            collective_id=0, has_side_effects=True, vmem_limit_bytes=int(63.0 * 1024 * 1024)
        ),
        cost_estimate=pl.CostEstimate(
            flops=8 * terms * block**3, bytes_accessed=4 * terms * block * block, transcendentals=0
        ),
    )(sector_sizes, term_links, wavefunction, left_env, right_env)
    return settle(first, second)


def solution(mesh):
    return jax.shard_map(
        functools.partial(on_device, mesh.shape["sec"]),
        mesh=mesh,
        in_specs=(
            P(("rep", "sec"), None, None),
            P(("rep", "sec"), None, None, None),
            P(("rep", "sec"), None, None, None),
            P("sec", None),
            P("sec", None),
        ),
        out_specs=(P(("rep", "sec"), None, None), P(("rep", "sec"), None, None)),
        check_vma=False,
    )
```
